32 devices in a mesh: groups: 2 (over y), outer: 4 (over z), inner: 2 (over x), heads: 2 (over core).
Axes of the slice: x: 2, y: 2, z: 4, core: 2. Of those that a mesh axis runs over, the one named last changes fastest.
Arguments:
- queries: bfloat16 [2048, 8192], P(('groups', 'outer', 'inner'), 'heads'), parts along dimension 0, may hold values from -4.5 to 4.5
- keys: bfloat16 [2048, 1024], P(('groups', 'outer', 'inner'), 'heads'), parts along dimension 0, may hold values from -4.5 to 4.5
- values: bfloat16 [2048, 1024], P(('groups', 'outer', 'inner'), 'heads'), parts along dimension 0, may hold values from -4.5 to 4.5
- prefix_keys: bfloat16 [128, 1024], P('groups', 'heads'), parts along dimension 0, may hold values from -5 to 5
- prefix_values: bfloat16 [128, 1024], P('groups', 'heads'), parts along dimension 0, may hold values from -4.5 to 4.5
Outputs:
- attended: bfloat16 [2048, 8192], P(('groups', 'outer', 'inner'), 'heads'), parts along dimension 0
The draws below stay inside these ranges and needn't reach their ends.
There are 2 independent parts, one for each index of `groups`. The reference program is written for one: setup_inputs(seed, part) draws one part's arguments, and reference() takes and returns one part's arrays. A program takes and returns all parts, laid end to end along the dimension named above; each array names one. Nothing has to cross between parts.
All inputs are finite; a program needn't handle non-finite values.
Results may differ from the reference program's by a relative error of at most 0.006.
Values may be sent and summed in bfloat16 or wider, within the bound.
A program may use at most 64 MiB of HBM per device.

```python
import jax
import jax.numpy as jnp
from jax import lax

HD = 128
KVH = 8
GQ = 8
PREFIX = 64
WINDOW = 256
BLOCK = 64
SEQ = 1024
N_OUTER = 4
N_INNER = 2


def draw_prefix_keys(key, part):
    base = jnp.clip(jax.random.normal(jax.random.fold_in(key, 23), (PREFIX, KVH * HD), jnp.float32), -4.5, 4.5)
    return base.astype(jnp.bfloat16)


def draw_queries(key, part):
    shape_full = (SEQ, KVH, GQ, HD)
    base = jnp.clip(jax.random.normal(jax.random.fold_in(key, 31), shape_full, jnp.float32), -4.5, 4.5)
    return base.reshape(SEQ, KVH * GQ * HD).astype(jnp.bfloat16)


def shard_levels(own_key, extent, split, low, top_value):
    def one(axis_at, blocks):
        heights = jax.random.uniform(jax.random.fold_in(jax.random.fold_in(own_key, 6), axis_at), (blocks,), jnp.float32, low / len(split), top_value / len(split))
        return jnp.repeat(jnp.exp(heights), extent[axis_at] // blocks).reshape((-1,) + (1,) * (len(extent) - axis_at - 1))

    loudness = one(*split[0])
    for cut in split[1:]:
        loudness = loudness * one(*cut)
    return loudness


def noise(rng, extent, scale, bound, split=(), held_as=jnp.bfloat16):
    values = jax.random.normal(rng, extent, jnp.float32) * scale
    if len(split) > 0:
        values = shard_levels(rng, extent, split, -0.22, 0.18) * values
    return jnp.clip(values, min=-bound, max=bound).astype(held_as)


def setup_inputs(seed: int = 0, part: int = 0) -> dict:
    seeds = jax.random.split(jax.random.key(seed), 6)
    part_splits = jax.random.split(jax.random.fold_in(seeds[5], part), 6)
    return {
        "queries": draw_queries(jax.random.fold_in(jax.random.fold_in(seeds[5], part), 71), part),
        "keys": noise(part_splits[1], (SEQ, KVH * HD), 1.0, 4.5, ((0, 8), (1, 2))),
        "values": noise(part_splits[2], (SEQ, KVH * HD), 1.0, 4.5, ((0, 8), (1, 2))),
        "prefix_keys": draw_prefix_keys(jax.random.fold_in(jax.random.fold_in(seeds[5], part), 71), part),
        "prefix_values": noise(part_splits[4], (PREFIX, KVH * HD), 1.0, 4.5, ((1, 2),)),
    }


def to_sequence(array_in):
    slot_count = N_OUTER * N_INNER
    grid = array_in.reshape(slot_count, 2, BLOCK, array_in.shape[1])
    return jnp.concatenate([grid[:, 0], grid[::-1, 1]], axis=0)


def from_sequence(blocks):
    slot_count = N_OUTER * N_INNER
    first = blocks[:slot_count]
    second = blocks[slot_count:][::-1]
    joined = jnp.stack([first, second], axis=1)
    return joined.reshape(slot_count * 2 * BLOCK, blocks.shape[2])


def reference(queries, keys, values, prefix_keys, prefix_values):
    slot_count = N_OUTER * N_INNER
    reach = WINDOW // BLOCK
    score_scale = 1.0 / (HD ** 0.5)
    seq_q = to_sequence(queries)
    seq_k = to_sequence(keys).reshape(2 * slot_count * BLOCK, KVH, HD)
    seq_v = to_sequence(values).reshape(2 * slot_count * BLOCK, KVH, HD)
    front = jnp.zeros((reach * BLOCK, KVH, HD), jnp.bfloat16)
    padded_k = jnp.concatenate([front, seq_k], axis=0)
    padded_v = jnp.concatenate([front, seq_v], axis=0)
    pre_k = prefix_keys.reshape(PREFIX, KVH, HD).astype(jnp.float32)
    pre_v = prefix_values.reshape(PREFIX, KVH, HD).astype(jnp.float32)
    span = (reach + 1) * BLOCK

    def one_block(block_index):
        start = (block_index * BLOCK).astype(jnp.int32)
        near_k = lax.dynamic_slice_in_dim(padded_k, start, span, 0).astype(jnp.float32)
        near_v = lax.dynamic_slice_in_dim(padded_v, start, span, 0).astype(jnp.float32)
        key_pos = start - reach * BLOCK + jnp.arange(span, dtype=jnp.int32)
        query_pos = start + jnp.arange(BLOCK, dtype=jnp.int32)
        query = seq_q[block_index].reshape(BLOCK, KVH, GQ, HD).astype(jnp.float32)
        local_s = jnp.einsum("rkgd,nkd->kgrn", query, near_k) * score_scale
        visible = (key_pos[None, :] >= 0) & (key_pos[None, :] <= query_pos[:, None]) & (key_pos[None, :] > query_pos[:, None] - WINDOW)
        local_s = jnp.where(visible[None, None], local_s, -jnp.inf)
        prefix_s = jnp.einsum("rkgd,nkd->kgrn", query, pre_k) * score_scale
        scores = jnp.concatenate([prefix_s, local_s], axis=-1)
        top_score = jnp.max(scores, axis=-1, keepdims=True)
        exps = jnp.exp(scores - top_score)
        total = jnp.sum(exps, axis=-1)
        rounded = lax.optimization_barrier(exps.astype(jnp.bfloat16)).astype(jnp.float32)
        both_v = jnp.concatenate([pre_v, near_v], axis=0)
        summed = jnp.einsum("kgrn,nkd->kgrd", rounded, both_v)
        result = summed / total[..., None]
        return result.transpose(2, 0, 1, 3).reshape(BLOCK, KVH * GQ * HD).astype(jnp.bfloat16)

    blocks = lax.map(one_block, jnp.arange(2 * slot_count, dtype=jnp.int32))
    return from_sequence(blocks)
```

```python
import functools

import jax
import jax.numpy as jnp
from jax import lax
from jax.experimental import pallas as pl
from jax.experimental.pallas import tpu as pltpu
from jax.sharding import PartitionSpec as P

HD = 128
GQ = 8
WINDOW = 256
LOG2E = 1.4426950408889634
MESH = pl.DeviceIdType.MESH


def kernel(
    slots, inner, heads, half, reach, prefix,
    q_hbm, k_hbm, v_hbm, pk_hbm, pv_hbm, o_hbm,
    q_v, kv, pre, o_v, q_sem, kv_sem, pre_sem, o_sem, send_sem, recv_sem,
):
    me = lax.axis_index("outer") * inner + lax.axis_index("inner")
    width = GQ * HD

    def load_kv(b, h, which):
        ref = (k_hbm, v_hbm)[which]
        return pltpu.make_async_copy(
            ref.at[pl.ds(b * half, half), pl.ds(h * HD, HD)],
            kv.at[b * (reach + 1), h, which],
            kv_sem.at[b, h, which],
        )

    def load_pre(h, which):
        ref = (pk_hbm, pv_hbm)[which]
        return pltpu.make_async_copy(ref.at[:, pl.ds(h * HD, HD)], pre.at[h, which], pre_sem.at[h, which])

    def load_q(h):
        return pltpu.make_async_copy(q_hbm.at[:, pl.ds(h * width, width)], q_v.at[h], q_sem.at[h])

    def store_o(h):
        return pltpu.make_async_copy(o_v.at[h], o_hbm.at[:, pl.ds(h * width, width)], o_sem.at[h])

    for h in range(heads):
        for b in range(2):
            for which in range(2):
                load_kv(b, h, which).start()
    for h in range(heads):
        load_q(h).start()
        load_pre(h, 0).start()
        load_pre(h, 1).start()

    sends = []
    for d in range(1, reach + 1):
        sends.append((me + d < slots, me + d, 0, d))
        sends.append((me - d >= 0, me - d, 1, reach + 1 + d))
        back = 2 * slots - 1 - me - d
        sends.append((back < me, back, 0, reach + 1 + d))
    receives = []
    for d in range(1, reach + 1):
        receives.append((me - d >= 0, me - d, d))
        receives.append((me + d < slots, me + d, reach + 1 + d))
        fold = 2 * slots - 1 - me - d
        receives.append(((fold > me) & (me + d >= slots), fold, reach + 1 + d))

    def place(slot):
        return {"outer": slot // inner, "inner": slot % inner}

    barrier = pltpu.get_barrier_semaphore()
    count = jnp.int32(0)
    for d in range(1, reach + 1):
        for valid, other in ((me + d < slots, me + d), (me - d >= 0, me - d)):
            count = count + valid.astype(jnp.int32)

            @pl.when(valid)
            def _():
                pl.semaphore_signal(barrier, inc=1, device_id=place(other), device_id_type=MESH)

    pl.semaphore_wait(barrier, count)

    def send(h, n):
        valid, partner, b, index = sends[n]
        return pltpu.make_async_remote_copy(
            src_ref=kv.at[b * (reach + 1), h],
            dst_ref=kv.at[index, h],
            send_sem=send_sem.at[h, n],
            recv_sem=recv_sem.at[h, index],
            device_id=place(partner),
            device_id_type=MESH,
        )

    for h in range(heads):
        for b in range(2):
            for which in range(2):
                load_kv(b, h, which).wait()
        for n in range(len(sends)):

            @pl.when(sends[n][0])
            def _():
                send(h, n).start()

    rows = lax.broadcasted_iota(jnp.int32, (half, half), 0)
    cols = lax.broadcasted_iota(jnp.int32, (half, half), 1)
    low = jnp.float32(-jnp.inf)
    causal = jnp.where(cols <= rows, 0.0, low)
    farthest = jnp.where(cols > rows, 0.0, low)

    def attend(h, b, blocks, biases):
        query = jnp.concatenate(
            [q_v[h, b * half : (b + 1) * half, g * HD : (g + 1) * HD] for g in range(GQ)], axis=0
        )
        keys = jnp.concatenate([pre[h, 0]] + [kv[i, h, 0] for i in blocks], axis=0)
        vals = jnp.concatenate([pre[h, 1]] + [kv[i, h, 1] for i in blocks], axis=0)
        vals = jnp.concatenate([vals, jnp.ones_like(vals)], axis=1)
        scores = lax.dot_general(query, keys, (((1,), (1,)), ((), ())), preferred_element_type=jnp.float32)
        scores = scores * (LOG2E / HD**0.5)
        bias = jnp.concatenate([jnp.zeros((half, prefix), jnp.float32)] + biases, axis=1)
        scores = (scores.reshape(GQ, half, -1) + bias[None]).reshape(GQ * half, -1)
        top = jnp.max(scores, axis=1, keepdims=True)
        weights = jnp.exp2(scores - top).astype(jnp.bfloat16)
        both = jnp.dot(weights, vals, preferred_element_type=jnp.float32)
        out = (both[:, :HD] / both[:, HD:]).astype(jnp.bfloat16)
        for g in range(GQ):
            o_v[h, b * half : (b + 1) * half, g * HD : (g + 1) * HD] = out[g * half : (g + 1) * half]

    def head(h, carry):
        load_q(h).wait()
        load_pre(h, 0).wait()
        load_pre(h, 1).wait()
        for valid, partner, index in receives:

            @pl.when(valid)
            def _():
                pltpu.make_async_remote_copy(
                    src_ref=kv.at[0, h],
                    dst_ref=kv.at[index, h],
                    send_sem=send_sem.at[h, 0],
                    recv_sem=recv_sem.at[h, index],
                    device_id=place(partner),
                    device_id_type=MESH,
                ).wait_recv()

        zero = jnp.zeros((half, half), jnp.float32)
        blocks, biases = [0], [causal]
        for d in range(1, reach + 1):
            there = me - d >= 0
            blocks.append(jnp.where(there, d, 0))
            biases.append(jnp.where(there, farthest if d == reach else zero, low))
        attend(h, 0, blocks, biases)
        blocks, biases = [reach + 1], [causal]
        for d in range(1, reach + 1):
            fold = 2 * slots - 1 - me - d
            blocks.append(jnp.where(fold <= me, me - fold, reach + 1 + d))
            biases.append(farthest if d == reach else zero)
        attend(h, 1, blocks, biases)
        store_o(h).start()
        return carry

    lax.fori_loop(0, heads, head, 0)
    for h in range(heads):
        store_o(h).wait()
        for n in range(len(sends)):

            @pl.when(sends[n][0])
            def _():
                send(h, n).wait_send()


def solution(mesh):
    inner = mesh.shape["inner"]
    slots = mesh.shape["outer"] * inner

    def local(q, k, v, pk, pv):
        rows, columns = k.shape
        heads, half, prefix = columns // HD, rows // 2, pk.shape[0]
        reach = WINDOW // half
        any_spec = pl.BlockSpec(memory_space=pl.ANY)
        scores = q.shape[0] * heads * GQ * (prefix + (reach + 1) * half)
        return pl.pallas_call(
            functools.partial(kernel, slots, inner, heads, half, reach, prefix),
            out_shape=jax.ShapeDtypeStruct(q.shape, jnp.bfloat16),
            in_specs=[any_spec] * 5,
            out_specs=any_spec,
            scratch_shapes=[
                pltpu.VMEM((heads, rows, GQ * HD), jnp.bfloat16),
                pltpu.VMEM((2 * (reach + 1), heads, 2, half, HD), jnp.bfloat16),
                pltpu.VMEM((heads, 2, prefix, HD), jnp.bfloat16),
                pltpu.VMEM((heads, rows, GQ * HD), jnp.bfloat16),
                pltpu.SemaphoreType.DMA((heads,)),
                pltpu.SemaphoreType.DMA((2, heads, 2)),
                pltpu.SemaphoreType.DMA((heads, 2)),
                pltpu.SemaphoreType.DMA((heads,)),
                pltpu.SemaphoreType.DMA((heads, 3 * reach)),
                pltpu.SemaphoreType.DMA((heads, 2 * (reach + 1))),
            ],
            compiler_params=pltpu.CompilerParams(
                collective_id=0, has_side_effects=True, vmem_limit_bytes=32 * 1024 * 1024
            ),
            cost_estimate=pl.CostEstimate(
                flops=scores * HD * 4, bytes_accessed=4 * q.size, transcendentals=scores
            ),
        )(q, k, v, pk, pv)

    placed = (
        P(("groups", "outer", "inner"), "heads"),
        P(("groups", "outer", "inner"), "heads"),
        P(("groups", "outer", "inner"), "heads"),
        P("groups", "heads"),
        P("groups", "heads"),
    )
    return jax.shard_map(
        local,
        mesh=mesh,
        in_specs=placed,
        out_specs=P(("groups", "outer", "inner"), "heads"),
        check_vma=False,
    )
```

```python
import functools

import jax
import jax.numpy as jnp
from jax import lax
from jax.experimental import pallas as pl
from jax.experimental.pallas import tpu as pltpu
from jax.sharding import PartitionSpec as P

HD = 128
GQ = 8
WINDOW = 256
LOG2E = 1.4426950408889634
MESH = pl.DeviceIdType.MESH

TREES = {
    (0, 0): ((0, 2), (0, 1), (2, 4), (1, 3)),
    (1, 0): ((1, 3), (3, 5), (3, 2), (2, 4)),
    (1, 1): ((1, 0),),
    (2, 0): ((2, 4), (2, 3), (4, 6), (3, 5)),
    (2, 1): ((2, 0), (0, 1)),
    (3, 0): ((3, 5), (5, 7), (5, 4), (4, 6)),
    (3, 1): ((3, 1), (1, 0), (0, 2)),
    (4, 0): ((4, 6), (4, 5), (6, 7)),
    (4, 1): ((4, 2), (2, 0), (2, 3), (0, 1)),
    (5, 0): ((5, 7), (7, 6)),
    (5, 1): ((5, 3), (5, 4), (3, 1), (3, 2)),
    (6, 0): ((6, 7), (7, 5)),
    (6, 1): ((6, 4), (4, 2), (4, 5), (2, 3)),
    (7, 0): ((7, 5), (7, 6), (5, 4)),
    (7, 1): ((7, 5), (7, 6), (5, 3), (6, 4)),
}


class Route:
    def __init__(self, here):
        self.here = here
        self.own, self.relays, self.leaves, self.sends, self.partners = [], [], [], [], []

    def send(self, valid, source, partner, index):
        self.sends.append((valid, len(self.sends), source, partner, index))
        return self.sends[-1]


def programs(slots, inner, reach, me):
    def landing(slot, half, at):
        if slot == at:
            return half * (reach + 1)
        if half == 1:
            return reach + 1 + slot - at
        return at - slot if slot < at else reach + 1 + 2 * slots - 1 - at - slot

    if (slots, inner, reach) == (8, 2, 4):
        routes = []
        for at in range(slots):
            route = Route(me == at)
            depths = []
            for (slot, half), hops in TREES.items():
                depth = {slot: 0}
                for a, b in hops:
                    depth[b] = depth[a] + 1
                    for other in (a, b):
                        if at in (a, b) and other != at and (None, other) not in route.partners:
                            route.partners.append((None, other))
                index = landing(slot, half, at)
                sends = [route.send(None, index, b, landing(slot, half, b)) for a, b in hops if a == at]
                if slot == at:
                    route.own.extend(sends)
                elif at in depth and sends:
                    depths.append((depth[at], index, sends))
                elif at in depth:
                    route.leaves.append((None, index))
            route.relays = depths
            routes.append(route)
        return routes

    route = Route(None)
    for d in range(1, reach + 1):
        up, down = (me + d < slots, me + d), (me - d >= 0, me - d)
        route.partners += [up, down]
        route.own.append(route.send(*up[:1], 0, up[1], d))
        route.own.append(route.send(*down[:1], reach + 1, down[1], reach + 1 + d))
        route.leaves.append((down[0], d))
        fold = 2 * slots - 1 - me - d
        route.own.append(route.send(fold < me, 0, fold, reach + 1 + d))
        route.leaves.append((up[0] | (fold > me), reach + 1 + d))
    return [route]


def kernel(
    slots, inner, heads, half, reach, prefix,
    q_hbm, k_hbm, v_hbm, pk_hbm, pv_hbm, o_hbm,
    q_v, kv, pre, o_v, q_sem, kv_sem, pre_sem, o_sem, send_sem, recv_sem,
):
    me = lax.axis_index("outer") * inner + lax.axis_index("inner")
    width = GQ * HD

    def load_kv(b, h, which):
        ref = (k_hbm, v_hbm)[which]
        return pltpu.make_async_copy(
            ref.at[pl.ds(b * half, half), pl.ds(h * HD, HD)],
            kv.at[b * (reach + 1), h, which],
            kv_sem.at[b, h, which],
        )

    def load_pre(h, which):
        ref = (pk_hbm, pv_hbm)[which]
        return pltpu.make_async_copy(ref.at[:, pl.ds(h * HD, HD)], pre.at[h, which], pre_sem.at[h, which])

    def load_q(h):
        return pltpu.make_async_copy(q_hbm.at[:, pl.ds(h * width, width)], q_v.at[h], q_sem.at[h])

    def store_o(h):
        return pltpu.make_async_copy(o_v.at[h], o_hbm.at[:, pl.ds(h * width, width)], o_sem.at[h])

    for h in range(heads):
        for b in range(2):
            for which in range(2):
                load_kv(b, h, which).start()
    for h in range(heads):
        load_q(h).start()
        load_pre(h, 0).start()
        load_pre(h, 1).start()

    routes = programs(slots, inner, reach, me)

    def place(slot):
        return {"outer": slot // inner, "inner": slot % inner}

    def when(condition, body):
        if condition is None:
            body()
        else:
            pl.when(condition)(body)

    def copy(h, n, source, partner, index):
        return pltpu.make_async_remote_copy(
            src_ref=kv.at[source, h],
            dst_ref=kv.at[index, h],
            send_sem=send_sem.at[h, n],
            recv_sem=recv_sem.at[h, index],
            device_id=place(partner),
            device_id_type=MESH,
        )

    def start(h, sends):
        for valid, n, source, partner, index in sends:
            when(valid, lambda: copy(h, n, source, partner, index).start())

    def arrived(h, valid, index):
        when(valid, lambda: copy(h, 0, 0, 0, index).wait_recv())

    def greet(route):
        barrier = pltpu.get_barrier_semaphore()
        count = 0
        for valid, other in route.partners:
            count = count + (1 if valid is None else valid.astype(jnp.int32))
            when(
                valid,
                lambda: pl.semaphore_signal(barrier, inc=1, device_id=place(other), device_id_type=MESH),
            )
        pl.semaphore_wait(barrier, count)

    def each_route(body):
        for route in routes:
            when(route.here, lambda: body(route))

    each_route(greet)

    def own(h):
        for b in range(2):
            for which in range(2):
                load_kv(b, h, which).wait()
        each_route(lambda route: start(h, route.own))

    def relay(h, level):
        def body(route):
            for depth, index, sends in route.relays:
                if depth == level:
                    arrived(h, None, index)
                    start(h, sends)

        each_route(body)

    def leaves(h):
        def body(route):
            for valid, index in route.leaves:
                arrived(h, valid, index)

        each_route(body)

    def drain(h):
        def body(route):
            for valid, n, source, partner, index in route.sends:
                when(valid, lambda: copy(h, n, source, partner, index).wait_send())

        each_route(body)

    for h in range(heads):
        own(h)

    rows = lax.broadcasted_iota(jnp.int32, (half, half), 0)
    cols = lax.broadcasted_iota(jnp.int32, (half, half), 1)
    low = jnp.float32(-jnp.inf)
    causal = jnp.where(cols <= rows, 0.0, low)
    farthest = jnp.where(cols > rows, 0.0, low)

    def attend(h, b, blocks, biases):
        query = jnp.concatenate(
            [q_v[h, b * half : (b + 1) * half, g * HD : (g + 1) * HD] for g in range(GQ)], axis=0
        )
        keys = jnp.concatenate([pre[h, 0]] + [kv[i, h, 0] for i in blocks], axis=0)
        vals = jnp.concatenate([pre[h, 1]] + [kv[i, h, 1] for i in blocks], axis=0)
        vals = jnp.concatenate([vals, jnp.ones_like(vals)], axis=1)
        scores = lax.dot_general(query, keys, (((1,), (1,)), ((), ())), preferred_element_type=jnp.float32)
        scores = scores * (LOG2E / HD**0.5)
        bias = jnp.concatenate([jnp.zeros((half, prefix), jnp.float32)] + biases, axis=1)
        scores = (scores.reshape(GQ, half, -1) + bias[None]).reshape(GQ * half, -1)
        top = jnp.max(scores, axis=1, keepdims=True)
        weights = jnp.exp2(scores - top).astype(jnp.bfloat16)
        both = jnp.dot(weights, vals, preferred_element_type=jnp.float32)
        out = (both[:, :HD] / both[:, HD:]).astype(jnp.bfloat16)
        for g in range(GQ):
            o_hbm[b * half : (b + 1) * half, pl.ds(pl.multiple_of(h * width + g * HD, HD), HD)] = out[g * half : (g + 1) * half]

    def head(h):
        load_q(h).wait()
        load_pre(h, 0).wait()
        load_pre(h, 1).wait()
        leaves(h)

        zero = jnp.zeros((half, half), jnp.float32)
        blocks, biases = [0], [causal]
        for d in range(1, reach + 1):
            there = me - d >= 0
            blocks.append(jnp.where(there, d, 0))
            biases.append(jnp.where(there, farthest if d == reach else zero, low))
        attend(h, 0, blocks, biases)
        blocks, biases = [reach + 1], [causal]
        for d in range(1, reach + 1):
            fold = 2 * slots - 1 - me - d
            blocks.append(jnp.where(fold <= me, me - fold, reach + 1 + d))
            biases.append(farthest if d == reach else zero)
        attend(h, 1, blocks, biases)

    def step(h, carry):
        @pl.when(h < heads)
        def _():
            relay(h, 1)

        @pl.when((h >= 1) & (h <= heads))
        def _():
            relay(h - 1, 2)

        @pl.when(h >= 2)
        def _():
            head(h - 2)

        return carry

    lax.fori_loop(0, heads + 2, step, 0)
    for h in range(heads):
        drain(h)


def solution(mesh):
    inner = mesh.shape["inner"]
    slots = mesh.shape["outer"] * inner

    def local(q, k, v, pk, pv):
        rows, columns = k.shape
        heads, half, prefix = columns // HD, rows // 2, pk.shape[0]
        reach = WINDOW // half
        any_spec = pl.BlockSpec(memory_space=pl.ANY)
        scores = q.shape[0] * heads * GQ * (prefix + (reach + 1) * half)
        return pl.pallas_call(
            functools.partial(kernel, slots, inner, heads, half, reach, prefix),
            out_shape=pltpu.VMEM(q.shape, jnp.bfloat16),
            in_specs=[any_spec] * 5,
            out_specs=pl.BlockSpec(memory_space=pltpu.VMEM),
            scratch_shapes=[
                pltpu.VMEM((heads, rows, GQ * HD), jnp.bfloat16),
                pltpu.VMEM((2 * (reach + 1), heads, 2, half, HD), jnp.bfloat16),
                pltpu.VMEM((heads, 2, prefix, HD), jnp.bfloat16),
                pltpu.VMEM((heads, rows, GQ * HD), jnp.bfloat16),
                pltpu.SemaphoreType.DMA((heads,)),
                pltpu.SemaphoreType.DMA((2, heads, 2)),
                pltpu.SemaphoreType.DMA((heads, 2)),
                pltpu.SemaphoreType.DMA((heads,)),
                pltpu.SemaphoreType.DMA((heads, 3 * reach)),
                pltpu.SemaphoreType.DMA((heads, 2 * (reach + 1))),
            ],
            compiler_params=pltpu.CompilerParams(
                collective_id=0, has_side_effects=True, vmem_limit_bytes=58 * 1024 * 1024
            ),
            cost_estimate=pl.CostEstimate(
                flops=scores * HD * 4, bytes_accessed=4 * q.size, transcendentals=scores
            ),
        )(q, k, v, pk, pv)

    placed = (
        P(("groups", "outer", "inner"), "heads"),
        P(("groups", "outer", "inner"), "heads"),
        P(("groups", "outer", "inner"), "heads"),
        P("groups", "heads"),
        P("groups", "heads"),
    )
    return jax.shard_map(
        local,
        mesh=mesh,
        in_specs=placed,
        out_specs=P(("groups", "outer", "inner"), "heads"),
        check_vma=False,
    )
```

```python
import functools

import jax
import jax.numpy as jnp
from jax import lax
from jax.experimental import pallas as pl
from jax.experimental.pallas import tpu as pltpu
from jax.sharding import PartitionSpec as P

HD = 128
GQ = 8
WINDOW = 256
LOG2E = 1.4426950408889634
MESH = pl.DeviceIdType.MESH

TREES = {
    (0, 0): ((0, 1), (0, 2), (1, 3), (2, 4)),
    (1, 0): ((1, 2), (1, 3), (2, 4), (3, 5)),
    (1, 1): ((1, 0),),
    (2, 0): ((2, 3), (2, 4), (3, 5), (4, 6)),
    (2, 1): ((2, 0), (0, 1)),
    (3, 0): ((3, 5), (5, 4), (5, 6), (5, 7)),
    (3, 1): ((3, 1), (3, 2), (1, 0)),
    (4, 0): ((4, 6), (4, 5), (6, 7)),
    (4, 1): ((4, 2), (2, 0), (2, 1), (2, 3)),
    (5, 0): ((5, 6), (5, 7)),
    (5, 1): ((5, 3), (5, 4), (3, 1), (3, 2)),
    (6, 0): ((6, 7), (7, 5)),
    (6, 1): ((6, 4), (4, 2), (4, 3), (4, 5)),
    (7, 0): ((7, 6), (7, 5), (6, 4)),
    (7, 1): ((7, 5), (7, 6), (5, 3), (6, 4)),
}


class Route:
    def __init__(self, here):
        self.here = here
        self.own, self.relays, self.leaves, self.sends, self.partners = [], [], [], [], []
        self.deep = []

    def send(self, valid, source, partner, index):
        self.sends.append((valid, len(self.sends), source, partner, index))
        return self.sends[-1]


def programs(slots, inner, reach, me):
    def landing(slot, half, at):
        if slot == at:
            return half * (reach + 1)
        if half == 1:
            return reach + 1 + slot - at
        return at - slot if slot < at else reach + 1 + 2 * slots - 1 - at - slot

    if (slots, inner, reach) == (8, 2, 4):
        routes = []
        for at in range(slots):
            route = Route(me == at)
            depths = []
            for (slot, half), hops in TREES.items():
                depth = {slot: 0}
                for a, b in hops:
                    depth[b] = depth[a] + 1
                    for other in (a, b):
                        if at in (a, b) and other != at and (None, other) not in route.partners:
                            route.partners.append((None, other))
                index = landing(slot, half, at)
                sends = [route.send(None, index, b, landing(slot, half, b)) for a, b in hops if a == at]
                if slot == at:
                    passing = {a for a, b in hops}
                    for entry in sends:
                        (route.deep if entry[3] in passing else route.own).append(entry)
                elif at in depth and sends:
                    depths.append((depth[at], index, sends))
                elif at in depth:
                    route.leaves.append((None, index))
            route.relays = depths
            routes.append(route)
        return routes

    route = Route(None)
    for d in range(1, reach + 1):
        up, down = (me + d < slots, me + d), (me - d >= 0, me - d)
        route.partners += [up, down]
        route.own.append(route.send(*up[:1], 0, up[1], d))
        route.own.append(route.send(*down[:1], reach + 1, down[1], reach + 1 + d))
        route.leaves.append((down[0], d))
        fold = 2 * slots - 1 - me - d
        route.own.append(route.send(fold < me, 0, fold, reach + 1 + d))
        route.leaves.append((up[0] | (fold > me), reach + 1 + d))
    return [route]


def kernel(
    slots, inner, heads, half, reach, prefix,
    q_hbm, k_hbm, v_hbm, pk_hbm, pv_hbm, o_hbm,
    q_v, kv, pre, o_v, q_sem, kv_sem, pre_sem, o_sem, send_sem, recv_sem,
):
    me = lax.axis_index("outer") * inner + lax.axis_index("inner")
    width = GQ * HD

    def load_kv(b, h, which):
        ref = (k_hbm, v_hbm)[which]
        return pltpu.make_async_copy(
            ref.at[pl.ds(b * half, half), pl.ds(h * HD, HD)],
            kv.at[b * (reach + 1), h, which],
            kv_sem.at[b, h, which],
        )

    def load_pre(h, which):
        ref = (pk_hbm, pv_hbm)[which]
        return pltpu.make_async_copy(ref.at[:, pl.ds(h * HD, HD)], pre.at[h, which], pre_sem.at[h, which])

    def load_q(h):
        return pltpu.make_async_copy(q_hbm.at[:, pl.ds(h * width, width)], q_v.at[h], q_sem.at[h])

    def store_o(h):
        return pltpu.make_async_copy(o_v.at[h], o_hbm.at[:, pl.ds(h * width, width)], o_sem.at[h])

    routes = programs(slots, inner, reach, me)

    def place(slot):
        return {"outer": slot // inner, "inner": slot % inner}

    def when(condition, body):
        if condition is None:
            body()
        else:
            pl.when(condition)(body)

    def copy(h, n, source, partner, index):
        return pltpu.make_async_remote_copy(
            src_ref=kv.at[source, h],
            dst_ref=kv.at[index, h],
            send_sem=send_sem.at[h, n],
            recv_sem=recv_sem.at[h, index],
            device_id=place(partner),
            device_id_type=MESH,
        )

    def start(h, sends):
        for valid, n, source, partner, index in sends:
            when(valid, lambda: copy(h, n, source, partner, index).start())

    def arrived(h, valid, index):
        when(valid, lambda: copy(h, 0, 0, 0, index).wait_recv())

    def greet(route):
        barrier = pltpu.get_barrier_semaphore()
        for valid, other in route.partners:
            when(
                valid,
                lambda: pl.semaphore_signal(barrier, inc=1, device_id=place(other), device_id_type=MESH),
            )

    def each_route(body):
        for route in routes:
            when(route.here, lambda: body(route))

    def all_here(route):
        pl.semaphore_wait(pltpu.get_barrier_semaphore(), greetings(route))

    def greetings(route):
        return sum(1 if valid is None else valid.astype(jnp.int32) for valid, _ in route.partners)

    each_route(greet)
    for h in range(heads):
        for b in range(2):
            for which in range(2):
                load_kv(b, h, which).start()
    each_route(all_here)

    def own(h):
        for b in range(2):
            for which in range(2):
                load_kv(b, h, which).wait()
        each_route(lambda route: start(h, route.deep))

    def own_leaves(h):
        each_route(lambda route: start(h, route.own))

    def relay(h, level):
        def body(route):
            for depth, index, sends in route.relays:
                if depth == level:
                    arrived(h, None, index)
                    start(h, sends)

        each_route(body)

    def leaves(h):
        def body(route):
            for valid, index in route.leaves:
                arrived(h, valid, index)

        each_route(body)

    def drain(h):
        def body(route):
            for valid, n, source, partner, index in route.sends:
                when(valid, lambda: copy(h, n, source, partner, index).wait_send())

        each_route(body)

    for h in range(heads):
        own(h)
    for h in range(heads):
        load_q(h).start()
        load_pre(h, 0).start()
        load_pre(h, 1).start()

    rows = lax.broadcasted_iota(jnp.int32, (half, half), 0)
    cols = lax.broadcasted_iota(jnp.int32, (half, half), 1)
    low = jnp.float32(-jnp.inf)
    causal = jnp.where(cols <= rows, 0.0, low)
    farthest = jnp.where(cols > rows, 0.0, low)

    def attend(h, b, blocks, biases):
        query = jnp.concatenate(
            [q_v[h, b * half : (b + 1) * half, g * HD : (g + 1) * HD] for g in range(GQ)], axis=0
        )
        keys = jnp.concatenate([pre[h, 0]] + [kv[i, h, 0] for i in blocks], axis=0)
        vals = jnp.concatenate([pre[h, 1]] + [kv[i, h, 1] for i in blocks], axis=0)
        vals = jnp.concatenate([vals, jnp.ones_like(vals)], axis=1)
        scores = lax.dot_general(query, keys, (((1,), (1,)), ((), ())), preferred_element_type=jnp.float32)
        scores = scores * (LOG2E / HD**0.5)
        bias = jnp.concatenate([jnp.zeros((half, prefix), jnp.float32)] + biases, axis=1)
        scores = (scores.reshape(GQ, half, -1) + bias[None]).reshape(GQ * half, -1)
        top = jnp.max(scores, axis=1, keepdims=True)
        weights = jnp.exp2(scores - top).astype(jnp.bfloat16)
        both = jnp.dot(weights, vals, preferred_element_type=jnp.float32)
        out = (both[:, :HD] / both[:, HD:]).astype(jnp.bfloat16)
        for g in range(GQ):
            o_hbm[b * half : (b + 1) * half, pl.ds(pl.multiple_of(h * width + g * HD, HD), HD)] = out[g * half : (g + 1) * half]

    def head(h):
        load_q(h).wait()
        load_pre(h, 0).wait()
        load_pre(h, 1).wait()
        leaves(h)

        zero = jnp.zeros((half, half), jnp.float32)
        blocks, biases = [0], [causal]
        for d in range(1, reach + 1):
            there = me - d >= 0
            blocks.append(jnp.where(there, d, 0))
            biases.append(jnp.where(there, farthest if d == reach else zero, low))
        attend(h, 0, blocks, biases)
        blocks, biases = [reach + 1], [causal]
        for d in range(1, reach + 1):
            fold = 2 * slots - 1 - me - d
            blocks.append(jnp.where(fold <= me, me - fold, reach + 1 + d))
            biases.append(farthest if d == reach else zero)
        attend(h, 1, blocks, biases)

    def step(h, carry):
        @pl.when(h < heads)
        def _():
            relay(h, 1)

        @pl.when(h < heads)
        def _():
            own_leaves(h)

        @pl.when(h >= 1)
        def _():
            head(h - 1)

        return carry

    lax.fori_loop(0, heads + 1, step, 0)
    for h in range(heads):
        drain(h)


def solution(mesh):
    inner = mesh.shape["inner"]
    slots = mesh.shape["outer"] * inner

    def local(q, k, v, pk, pv):
        rows, columns = k.shape
        heads, half, prefix = columns // HD, rows // 2, pk.shape[0]
        reach = WINDOW // half
        any_spec = pl.BlockSpec(memory_space=pl.ANY)
        scores = q.shape[0] * heads * GQ * (prefix + (reach + 1) * half)
        return pl.pallas_call(
            functools.partial(kernel, slots, inner, heads, half, reach, prefix),
            out_shape=pltpu.VMEM(q.shape, jnp.bfloat16),
            in_specs=[any_spec] * 5,
            out_specs=pl.BlockSpec(memory_space=pltpu.VMEM),
            scratch_shapes=[
                pltpu.VMEM((heads, rows, GQ * HD), jnp.bfloat16),
                pltpu.VMEM((2 * (reach + 1), heads, 2, half, HD), jnp.bfloat16),
                pltpu.VMEM((heads, 2, prefix, HD), jnp.bfloat16),
                pltpu.VMEM((heads, rows, GQ * HD), jnp.bfloat16),
                pltpu.SemaphoreType.DMA((heads,)),
                pltpu.SemaphoreType.DMA((2, heads, 2)),
                pltpu.SemaphoreType.DMA((heads, 2)),
                pltpu.SemaphoreType.DMA((heads,)),
                pltpu.SemaphoreType.DMA((heads, 3 * reach)),
                pltpu.SemaphoreType.DMA((heads, 2 * (reach + 1))),
            ],
            compiler_params=pltpu.CompilerParams(
                collective_id=0, has_side_effects=True, vmem_limit_bytes=58 * 1024 * 1024
            ),
            cost_estimate=pl.CostEstimate(
                flops=scores * HD * 4, bytes_accessed=4 * q.size, transcendentals=scores
            ),
        )(q, k, v, pk, pv)

    placed = (
        P(("groups", "outer", "inner"), "heads"),
        P(("groups", "outer", "inner"), "heads"),
        P(("groups", "outer", "inner"), "heads"),
        P("groups", "heads"),
        P("groups", "heads"),
    )
    return jax.shard_map(
        local,
        mesh=mesh,
        in_specs=placed,
        out_specs=P(("groups", "outer", "inner"), "heads"),
        check_vma=False,
    )
```

```python
import functools

import jax
import jax.numpy as jnp
from jax import lax
from jax.experimental import pallas as pl
from jax.experimental.pallas import tpu as pltpu
from jax.sharding import PartitionSpec as P

HD = 128
GQ = 8
WINDOW = 256
LOG2E = 1.4426950408889634
MESH = pl.DeviceIdType.MESH

TREES = {
    (0, 0): ((0, 1), (0, 2), (1, 3), (2, 4)),
    (1, 0): ((1, 2), (1, 3), (2, 4), (3, 5)),
    (1, 1): ((1, 0),),
    (2, 0): ((2, 3), (2, 4), (3, 5), (4, 6)),
    (2, 1): ((2, 0), (0, 1)),
    (3, 0): ((3, 5), (5, 4), (5, 6), (5, 7)),
    (3, 1): ((3, 1), (3, 2), (1, 0)),
    (4, 0): ((4, 6), (4, 5), (6, 7)),
    (4, 1): ((4, 2), (2, 0), (2, 1), (2, 3)),
    (5, 0): ((5, 6), (5, 7)),
    (5, 1): ((5, 3), (5, 4), (3, 1), (3, 2)),
    (6, 0): ((6, 7), (7, 5)),
    (6, 1): ((6, 4), (4, 2), (4, 3), (4, 5)),
    (7, 0): ((7, 6), (7, 5), (6, 4)),
    (7, 1): ((7, 5), (7, 6), (5, 3), (6, 4)),
}


class Route:
    def __init__(self, here):
        self.here = here
        self.own, self.relays, self.leaves, self.sends, self.partners = [], [], [], [], []
        self.deep = []

    def send(self, valid, source, partner, index):
        self.sends.append((valid, len(self.sends), source, partner, index))
        return self.sends[-1]


def programs(slots, inner, reach, me):
    def landing(slot, half, at):
        if slot == at:
            return half * (reach + 1)
        if half == 1:
            return reach + 1 + slot - at
        return at - slot if slot < at else reach + 1 + 2 * slots - 1 - at - slot

    if (slots, inner, reach) == (8, 2, 4):
        routes = []
        for at in range(slots):
            route = Route(me == at)
            depths = []
            for (slot, half), hops in TREES.items():
                depth = {slot: 0}
                for a, b in hops:
                    depth[b] = depth[a] + 1
                    for other in (a, b):
                        if at in (a, b) and other != at and (None, other) not in route.partners:
                            route.partners.append((None, other))
                index = landing(slot, half, at)
                sends = [route.send(None, index, b, landing(slot, half, b)) for a, b in hops if a == at]
                if slot == at:
                    passing = {a for a, b in hops}
                    for entry in sends:
                        (route.deep if entry[3] in passing else route.own).append(entry)
                elif at in depth and sends:
                    depths.append((depth[at], index, sends))
                elif at in depth:
                    route.leaves.append((None, index))
            route.relays = depths
            routes.append(route)
        return routes

    route = Route(None)
    for d in range(1, reach + 1):
        up, down = (me + d < slots, me + d), (me - d >= 0, me - d)
        route.partners += [up, down]
        route.own.append(route.send(*up[:1], 0, up[1], d))
        route.own.append(route.send(*down[:1], reach + 1, down[1], reach + 1 + d))
        route.leaves.append((down[0], d))
        fold = 2 * slots - 1 - me - d
        route.own.append(route.send(fold < me, 0, fold, reach + 1 + d))
        route.leaves.append((up[0] | (fold > me), reach + 1 + d))
    return [route]


def kernel(
    slots, inner, heads, half, reach, prefix,
    q_hbm, k_hbm, v_hbm, pk_hbm, pv_hbm, o_hbm,
    q_v, kv, pre, o_v, q_sem, kv_sem, pre_sem, o_sem, send_sem, recv_sem,
):
    me = lax.axis_index("outer") * inner + lax.axis_index("inner")
    width = GQ * HD

    def load_kv(b, h, which):
        ref = (k_hbm, v_hbm)[which]
        return pltpu.make_async_copy(
            ref.at[pl.ds(b * half, half), pl.ds(h * HD, HD)],
            kv.at[b * (reach + 1), h, which],
            kv_sem.at[b, h, which],
        )

    def load_pre(h, which):
        ref = (pk_hbm, pv_hbm)[which]
        return pltpu.make_async_copy(ref.at[:, pl.ds(h * HD, HD)], pre.at[h, which], pre_sem.at[h, which])

    def load_q(h):
        return pltpu.make_async_copy(q_hbm.at[:, pl.ds(h * width, width)], q_v.at[h], q_sem.at[h])

    def store_o(h):
        return pltpu.make_async_copy(o_v.at[h], o_hbm.at[:, pl.ds(h * width, width)], o_sem.at[h])

    routes = programs(slots, inner, reach, me)

    def place(slot):
        return {"outer": slot // inner, "inner": slot % inner}

    def when(condition, body):
        if condition is None:
            body()
        else:
            pl.when(condition)(body)

    def copy(h, n, source, partner, index):
        return pltpu.make_async_remote_copy(
            src_ref=kv.at[source, h],
            dst_ref=kv.at[index, h],
            send_sem=send_sem.at[h, n],
            recv_sem=recv_sem.at[h, index],
            device_id=place(partner),
            device_id_type=MESH,
        )

    def start(h, sends):
        for valid, n, source, partner, index in sends:
            when(valid, lambda: copy(h, n, source, partner, index).start())

    def arrived(h, valid, index):
        when(valid, lambda: copy(h, 0, 0, 0, index).wait_recv())

    def greet(route):
        barrier = pltpu.get_barrier_semaphore()
        for valid, other in route.partners:
            when(
                valid,
                lambda: pl.semaphore_signal(barrier, inc=1, device_id=place(other), device_id_type=MESH),
            )

    def each_route(body):
        for route in routes:
            when(route.here, lambda: body(route))

    def all_here(route):
        pl.semaphore_wait(pltpu.get_barrier_semaphore(), greetings(route))

    def greetings(route):
        return sum(1 if valid is None else valid.astype(jnp.int32) for valid, _ in route.partners)

    each_route(greet)
    for h in range(heads):
        for b in range(2):
            for which in range(2):
                load_kv(b, h, which).start()
    each_route(all_here)

    def own(h):
        for b in range(2):
            for which in range(2):
                load_kv(b, h, which).wait()
        each_route(lambda route: start(h, route.deep))

    def own_leaves(h):
        each_route(lambda route: start(h, route.own))

    def relay(h, level):
        def body(route):
            for depth, index, sends in route.relays:
                if depth == level:
                    arrived(h, None, index)
                    start(h, sends)

        each_route(body)

    def leaves(h):
        def body(route):
            for valid, index in route.leaves:
                arrived(h, valid, index)

        each_route(body)

    def drain(h):
        def body(route):
            for valid, n, source, partner, index in route.sends:
                when(valid, lambda: copy(h, n, source, partner, index).wait_send())

        each_route(body)

    for h in range(heads):
        own(h)
    for h in range(heads):
        load_q(h).start()
        load_pre(h, 0).start()
        load_pre(h, 1).start()

    rows = lax.broadcasted_iota(jnp.int32, (half, half), 0)
    cols = lax.broadcasted_iota(jnp.int32, (half, half), 1)
    low = jnp.float32(-jnp.inf)
    causal = jnp.where(cols <= rows, 0.0, low)
    farthest = jnp.where(cols > rows, 0.0, low)

    def attend(h, b, blocks, biases):
        query = jnp.concatenate(
            [q_v[h, b * half : (b + 1) * half, g * HD : (g + 1) * HD] for g in range(GQ)], axis=0
        )
        keys = jnp.concatenate([pre[h, 0]] + [kv[i, h, 0] for i in blocks], axis=0)
        vals = jnp.concatenate([pre[h, 1]] + [kv[i, h, 1] for i in blocks], axis=0)
        vals = jnp.concatenate([vals, jnp.ones_like(vals)], axis=1)
        scores = lax.dot_general(query, keys, (((1,), (1,)), ((), ())), preferred_element_type=jnp.float32)
        scores = scores * (LOG2E / HD**0.5)
        bias = jnp.concatenate([jnp.zeros((half, prefix), jnp.float32)] + biases, axis=1)
        scores = (scores.reshape(GQ, half, -1) + bias[None]).reshape(GQ * half, -1)
        top = jnp.max(scores, axis=1, keepdims=True)
        weights = jnp.exp2(scores - top).astype(jnp.bfloat16)
        both = jnp.dot(weights, vals, preferred_element_type=jnp.float32)
        out = (both[:, :HD] / both[:, HD:]).astype(jnp.bfloat16)
        for g in range(GQ):
            o_hbm[b * half : (b + 1) * half, pl.ds(pl.multiple_of(h * width + g * HD, HD), HD)] = out[g * half : (g + 1) * half]

    def head(h):
        load_q(h).wait()
        load_pre(h, 0).wait()
        load_pre(h, 1).wait()
        leaves(h)

        zero = jnp.zeros((half, half), jnp.float32)
        blocks, biases = [0], [causal]
        for d in range(1, reach + 1):
            there = me - d >= 0
            blocks.append(jnp.where(there, d, 0))
            biases.append(jnp.where(there, farthest if d == reach else zero, low))
        attend(h, 0, blocks, biases)
        blocks, biases = [reach + 1], [causal]
        for d in range(1, reach + 1):
            fold = 2 * slots - 1 - me - d
            blocks.append(jnp.where(fold <= me, me - fold, reach + 1 + d))
            biases.append(farthest if d == reach else zero)
        attend(h, 1, blocks, biases)

    def step(h, carry):
        @pl.when(h < heads)
        def _():
            relay(h, 1)

        @pl.when(h < heads)
        def _():
            own_leaves(h)

        @pl.when(h >= 3)
        def _():
            head(h - 3)

        return carry

    lax.fori_loop(0, heads + 3, step, 0)
    for h in range(heads):
        drain(h)


def solution(mesh):
    inner = mesh.shape["inner"]
    slots = mesh.shape["outer"] * inner

    def local(q, k, v, pk, pv):
        rows, columns = k.shape
        heads, half, prefix = columns // HD, rows // 2, pk.shape[0]
        reach = WINDOW // half
        any_spec = pl.BlockSpec(memory_space=pl.ANY)
        scores = q.shape[0] * heads * GQ * (prefix + (reach + 1) * half)
        return pl.pallas_call(
            functools.partial(kernel, slots, inner, heads, half, reach, prefix),
            out_shape=pltpu.VMEM(q.shape, jnp.bfloat16),
            in_specs=[any_spec] * 5,
            out_specs=pl.BlockSpec(memory_space=pltpu.VMEM),
            scratch_shapes=[
                pltpu.VMEM((heads, rows, GQ * HD), jnp.bfloat16),
                pltpu.VMEM((2 * (reach + 1), heads, 2, half, HD), jnp.bfloat16),
                pltpu.VMEM((heads, 2, prefix, HD), jnp.bfloat16),
                pltpu.VMEM((heads, rows, GQ * HD), jnp.bfloat16),
                pltpu.SemaphoreType.DMA((heads,)),
                pltpu.SemaphoreType.DMA((2, heads, 2)),
                pltpu.SemaphoreType.DMA((heads, 2)),
                pltpu.SemaphoreType.DMA((heads,)),
                pltpu.SemaphoreType.DMA((heads, 3 * reach)),
                pltpu.SemaphoreType.DMA((heads, 2 * (reach + 1))),
            ],
            compiler_params=pltpu.CompilerParams(
                collective_id=0, has_side_effects=True, vmem_limit_bytes=58 * 1024 * 1024
            ),
            cost_estimate=pl.CostEstimate(
                flops=scores * HD * 4, bytes_accessed=4 * q.size, transcendentals=scores
            ),
        )(q, k, v, pk, pv)

    placed = (
        P(("groups", "outer", "inner"), "heads"),
        P(("groups", "outer", "inner"), "heads"),
        P(("groups", "outer", "inner"), "heads"),
        P("groups", "heads"),
        P("groups", "heads"),
    )
    return jax.shard_map(
        local,
        mesh=mesh,
        in_specs=placed,
        out_specs=P(("groups", "outer", "inner"), "heads"),
        check_vma=False,
    )
```

```python
import functools

import jax
import jax.numpy as jnp
from jax import lax
from jax.experimental import pallas as pl
from jax.experimental.pallas import tpu as pltpu
from jax.sharding import PartitionSpec as P

HD = 128
GQ = 8
WINDOW = 256
LOG2E = 1.4426950408889634
MESH = pl.DeviceIdType.MESH

TREES = {
    (0, 0): ((0, 1), (0, 2), (1, 3), (2, 4)),
    (1, 0): ((1, 2), (1, 3), (2, 4), (3, 5)),
    (1, 1): ((1, 0),),
    (2, 0): ((2, 3), (2, 4), (3, 5), (4, 6)),
    (2, 1): ((2, 0), (0, 1)),
    (3, 0): ((3, 5), (5, 4), (5, 6), (5, 7)),
    (3, 1): ((3, 1), (3, 2), (1, 0)),
    (4, 0): ((4, 6), (4, 5), (6, 7)),
    (4, 1): ((4, 2), (2, 0), (2, 1), (2, 3)),
    (5, 0): ((5, 6), (5, 7)),
    (5, 1): ((5, 3), (5, 4), (3, 1), (3, 2)),
    (6, 0): ((6, 7), (7, 5)),
    (6, 1): ((6, 4), (4, 2), (4, 3), (4, 5)),
    (7, 0): ((7, 6), (7, 5), (6, 4)),
    (7, 1): ((7, 5), (7, 6), (5, 3), (6, 4)),
}


class Route:
    def __init__(self, here):
        self.here = here
        self.own, self.relays, self.leaves, self.sends, self.partners = [], [], [], [], []
        self.deep = []

    def send(self, valid, source, partner, index):
        self.sends.append((valid, len(self.sends), source, partner, index))
        return self.sends[-1]


def programs(slots, inner, reach, me):
    def landing(slot, half, at):
        if slot == at:
            return half * (reach + 1)
        if half == 1:
            return reach + 1 + slot - at
        return at - slot if slot < at else reach + 1 + 2 * slots - 1 - at - slot

    if (slots, inner, reach) == (8, 2, 4):
        routes = []
        for at in range(slots):
            route = Route(me == at)
            depths = []
            for (slot, half), hops in TREES.items():
                depth = {slot: 0}
                for a, b in hops:
                    depth[b] = depth[a] + 1
                    for other in (a, b):
                        if at in (a, b) and other != at and (None, other) not in route.partners:
                            route.partners.append((None, other))
                index = landing(slot, half, at)
                sends = [route.send(None, index, b, landing(slot, half, b)) for a, b in hops if a == at]
                if slot == at:
                    passing = {a for a, b in hops}
                    for entry in sends:
                        (route.deep if entry[3] in passing else route.own).append(entry)
                elif at in depth and sends:
                    depths.append((depth[at], index, sends))
                elif at in depth:
                    route.leaves.append((None, index))
            route.relays = depths
            routes.append(route)
        return routes

    route = Route(None)
    for d in range(1, reach + 1):
        up, down = (me + d < slots, me + d), (me - d >= 0, me - d)
        route.partners += [up, down]
        route.own.append(route.send(*up[:1], 0, up[1], d))
        route.own.append(route.send(*down[:1], reach + 1, down[1], reach + 1 + d))
        route.leaves.append((down[0], d))
        fold = 2 * slots - 1 - me - d
        route.own.append(route.send(fold < me, 0, fold, reach + 1 + d))
        route.leaves.append((up[0] | (fold > me), reach + 1 + d))
    return [route]


def kernel(
    slots, inner, heads, half, reach, prefix,
    q_hbm, k_hbm, v_hbm, pk_hbm, pv_hbm, o_hbm,
    q_v, kv, pre, o_v, q_sem, kv_sem, pre_sem, o_sem, send_sem, recv_sem,
):
    me = lax.axis_index("outer") * inner + lax.axis_index("inner")
    width = GQ * HD

    def load_kv(b, h, which):
        ref = (k_hbm, v_hbm)[which]
        return pltpu.make_async_copy(
            ref.at[pl.ds(b * half, half), pl.ds(h * HD, HD)],
            kv.at[b * (reach + 1), h, which],
            kv_sem.at[b, h, which],
        )

    def load_pre(h, which):
        ref = (pk_hbm, pv_hbm)[which]
        return pltpu.make_async_copy(ref.at[:, pl.ds(h * HD, HD)], pre.at[h, which], pre_sem.at[h, which])

    def load_q(h):
        return pltpu.make_async_copy(q_hbm.at[:, pl.ds(h * width, width)], q_v.at[h], q_sem.at[h])

    def store_o(h):
        return pltpu.make_async_copy(o_v.at[h], o_hbm.at[:, pl.ds(h * width, width)], o_sem.at[h])

    routes = programs(slots, inner, reach, me)

    def place(slot):
        return {"outer": slot // inner, "inner": slot % inner}

    def when(condition, body):
        if condition is None:
            body()
        else:
            pl.when(condition)(body)

    def copy(h, n, source, partner, index):
        return pltpu.make_async_remote_copy(
            src_ref=kv.at[source, h],
            dst_ref=kv.at[index, h],
            send_sem=send_sem.at[h, n],
            recv_sem=recv_sem.at[h, index],
            device_id=place(partner),
            device_id_type=MESH,
        )

    def start(h, sends):
        for valid, n, source, partner, index in sends:
            when(valid, lambda: copy(h, n, source, partner, index).start())

    def arrived(h, valid, index):
        when(valid, lambda: copy(h, 0, 0, 0, index).wait_recv())

    def greet(route):
        barrier = pltpu.get_barrier_semaphore()
        for valid, other in route.partners:
            when(
                valid,
                lambda: pl.semaphore_signal(barrier, inc=1, device_id=place(other), device_id_type=MESH),
            )

    def each_route(body):
        for route in routes:
            when(route.here, lambda: body(route))

    def all_here(route):
        pl.semaphore_wait(pltpu.get_barrier_semaphore(), greetings(route))

    def greetings(route):
        return sum(1 if valid is None else valid.astype(jnp.int32) for valid, _ in route.partners)

    each_route(greet)
    for h in range(heads):
        for b in range(2):
            for which in range(2):
                load_kv(b, h, which).start()
    each_route(all_here)

    def own(h):
        for b in range(2):
            for which in range(2):
                load_kv(b, h, which).wait()
        each_route(lambda route: start(h, route.deep))

    def own_leaves(h):
        each_route(lambda route: start(h, route.own))

    def relay(h, level):
        def body(route):
            for depth, index, sends in route.relays:
                if depth == level:
                    arrived(h, None, index)
                    start(h, sends)

        each_route(body)

    def leaves(h, second):
        def body(route):
            for valid, index in route.leaves:
                if (index > reach) == second:
                    arrived(h, valid, index)

        each_route(body)

    def drain(h):
        def body(route):
            for valid, n, source, partner, index in route.sends:
                when(valid, lambda: copy(h, n, source, partner, index).wait_send())

        each_route(body)

    for h in range(heads):
        own(h)
    for h in range(heads):
        load_q(h).start()
        load_pre(h, 0).start()
        load_pre(h, 1).start()

    rows = lax.broadcasted_iota(jnp.int32, (half, half), 0)
    cols = lax.broadcasted_iota(jnp.int32, (half, half), 1)
    low = jnp.float32(-jnp.inf)
    causal = jnp.where(cols <= rows, 0.0, low)
    farthest = jnp.where(cols > rows, 0.0, low)

    def attend(h, b, blocks, biases):
        query = jnp.concatenate(
            [q_v[h, b * half : (b + 1) * half, g * HD : (g + 1) * HD] for g in range(GQ)], axis=0
        )
        keys = jnp.concatenate([pre[h, 0]] + [kv[i, h, 0] for i in blocks], axis=0)
        vals = jnp.concatenate([pre[h, 1]] + [kv[i, h, 1] for i in blocks], axis=0)
        vals = jnp.concatenate([vals, jnp.ones_like(vals)], axis=1)
        scores = lax.dot_general(query, keys, (((1,), (1,)), ((), ())), preferred_element_type=jnp.float32)
        scores = scores * (LOG2E / HD**0.5)
        bias = jnp.concatenate([jnp.zeros((half, prefix), jnp.float32)] + biases, axis=1)
        scores = (scores.reshape(GQ, half, -1) + bias[None]).reshape(GQ * half, -1)
        top = jnp.max(scores, axis=1, keepdims=True)
        weights = jnp.exp2(scores - top).astype(jnp.bfloat16)
        both = jnp.dot(weights, vals, preferred_element_type=jnp.float32)
        out = (both[:, :HD] / both[:, HD:]).astype(jnp.bfloat16)
        for g in range(GQ):
            o_hbm[b * half : (b + 1) * half, pl.ds(pl.multiple_of(h * width + g * HD, HD), HD)] = out[g * half : (g + 1) * half]

    def head(h):
        load_q(h).wait()
        load_pre(h, 0).wait()
        load_pre(h, 1).wait()
        leaves(h, False)

        zero = jnp.zeros((half, half), jnp.float32)
        blocks, biases = [0], [causal]
        for d in range(1, reach + 1):
            there = me - d >= 0
            blocks.append(jnp.where(there, d, 0))
            biases.append(jnp.where(there, farthest if d == reach else zero, low))
        attend(h, 0, blocks, biases)
        leaves(h, True)
        blocks, biases = [reach + 1], [causal]
        for d in range(1, reach + 1):
            fold = 2 * slots - 1 - me - d
            blocks.append(jnp.where(fold <= me, me - fold, reach + 1 + d))
            biases.append(farthest if d == reach else zero)
        attend(h, 1, blocks, biases)

    def step(h, carry):
        @pl.when(h < heads)
        def _():
            relay(h, 1)

        @pl.when(h < heads)
        def _():
            own_leaves(h)

        @pl.when(h >= 3)
        def _():
            head(h - 3)

        return carry

    lax.fori_loop(0, heads + 3, step, 0)
    for h in range(heads):
        drain(h)


def solution(mesh):
    inner = mesh.shape["inner"]
    slots = mesh.shape["outer"] * inner

    def local(q, k, v, pk, pv):
        rows, columns = k.shape
        heads, half, prefix = columns // HD, rows // 2, pk.shape[0]
        reach = WINDOW // half
        any_spec = pl.BlockSpec(memory_space=pl.ANY)
        scores = q.shape[0] * heads * GQ * (prefix + (reach + 1) * half)
        return pl.pallas_call(
            functools.partial(kernel, slots, inner, heads, half, reach, prefix),
            out_shape=pltpu.VMEM(q.shape, jnp.bfloat16),
            in_specs=[any_spec] * 5,
            out_specs=pl.BlockSpec(memory_space=pltpu.VMEM),
            scratch_shapes=[
                pltpu.VMEM((heads, rows, GQ * HD), jnp.bfloat16),
                pltpu.VMEM((2 * (reach + 1), heads, 2, half, HD), jnp.bfloat16),
                pltpu.VMEM((heads, 2, prefix, HD), jnp.bfloat16),
                pltpu.VMEM((heads, rows, GQ * HD), jnp.bfloat16),
                pltpu.SemaphoreType.DMA((heads,)),
                pltpu.SemaphoreType.DMA((2, heads, 2)),
                pltpu.SemaphoreType.DMA((heads, 2)),
                pltpu.SemaphoreType.DMA((heads,)),
                pltpu.SemaphoreType.DMA((heads, 3 * reach)),
                pltpu.SemaphoreType.DMA((heads, 2 * (reach + 1))),
            ],
            compiler_params=pltpu.CompilerParams(
                collective_id=0, has_side_effects=True, vmem_limit_bytes=58 * 1024 * 1024
            ),
            cost_estimate=pl.CostEstimate(
                flops=scores * HD * 4, bytes_accessed=4 * q.size, transcendentals=scores
            ),
        )(q, k, v, pk, pv)

    placed = (
        P(("groups", "outer", "inner"), "heads"),
        P(("groups", "outer", "inner"), "heads"),
        P(("groups", "outer", "inner"), "heads"),
        P("groups", "heads"),
        P("groups", "heads"),
    )
    return jax.shard_map(
        local,
        mesh=mesh,
        in_specs=placed,
        out_specs=P(("groups", "outer", "inner"), "heads"),
        check_vma=False,
    )
```
